32 devices in a mesh: shell: 4 (over z), sky: 8 (over y, x, core).
Axes of the slice: x: 2, y: 2, z: 4, core: 2. Of those that a mesh axis runs over, the one named last changes fastest.
Arguments:
- density: bfloat16 [100, 384, 384], P('shell', 'sky'), may hold values from -6 to 6
- kernel_table: float32 [16, 4], replicated, may hold values from 0.02 to 0.4
- shell_row: int32 [100], P('shell'), may hold values from 0 to 15, as said below
- theta_first: bfloat16 [6, 4, 64], replicated, may hold values from -1.25 to 1.25
- bias_first: float32 [64], replicated, may hold values from -3 to 3
- theta_second: bfloat16 [6, 64, 64], replicated, may hold values from -0.3125 to 0.3125
- bias_second: float32 [64], replicated, may hold values from -3 to 3
Outputs:
- features: bfloat16 [64, 384, 384], P('shell', 'sky')
The draws below stay inside these ranges and needn't reach their ends.
Inputs may be any that keep to these rules, and one draw needn't show every extreme that they name: `shell_row`: each shell names one row of kernel_table; both the first and the last row are named.
All inputs are finite; a program needn't handle non-finite values.
Results may differ from the reference program's by a relative error of at most 0.0062.
Values may be sent and summed in bfloat16 or wider, within the bound.
A program may use at most 128 MiB of HBM per device.

```python
import math
import jax
import jax.numpy as jnp
from jax import lax

BINS = 4
CH = 64
ORDER = 6
KROWS = 16
C = 384
SHELLS = 100
ROWS = 384


def draw_shell_row(key, part):
    picked = jax.random.randint(jax.random.fold_in(key, 11), (SHELLS,), 0, KROWS)
    position = jax.random.randint(jax.random.fold_in(key, 12), (), 0, SHELLS)
    picked = picked.at[position].set(KROWS - 1)
    picked = picked.at[(position + 1) % SHELLS].set(0)
    return picked.astype(jnp.int32)


def block_levels(rng, dims, shards, least, top_value):
    def one(dim, blocks):
        steps = jax.random.uniform(jax.random.fold_in(jax.random.fold_in(rng, 6), dim), (blocks,), jnp.float32, least / len(shards), top_value / len(shards))
        return jnp.repeat(jnp.exp(steps), dims[dim] // blocks).reshape((-1,) + (1,) * (len(dims) - dim - 1))

    factor_of = one(*shards[0])
    for cut in shards[1:]:
        factor_of = factor_of * one(*cut)
    return factor_of


def centred(key, dims, deviation, bound, shards=(), held_as=jnp.bfloat16):
    values = deviation * jax.random.normal(key, dims, jnp.float32)
    if shards:
        values = values * block_levels(key, dims, shards, -0.22, 0.18)
    return jnp.clip(values, -bound, bound).astype(held_as)


def setup_inputs(seed: int = 0) -> dict:
    key_of = jax.random.split(jax.random.key(seed), 8)
    return {
        "density": centred(key_of[0], (SHELLS, ROWS, C), 1.0, 6.0, ((0, 4), (1, 8))),
        "kernel_table": jnp.clip(jnp.exp(jax.random.uniform(key_of[1], (KROWS, BINS), jnp.float32, math.log(0.02), math.log(0.4))), 0.02, 0.4),
        "shell_row": draw_shell_row(jax.random.fold_in(key_of[7], 71), 0),
        "theta_first": centred(key_of[3], (ORDER, BINS, CH), (ORDER * BINS) ** -0.5, 1.25),
        "bias_first": centred(key_of[4], (CH,), 0.5, 3.0, (), jnp.float32),
        "theta_second": centred(key_of[5], (ORDER, CH, CH), (ORDER * CH) ** -0.5, 0.3125),
        "bias_second": centred(key_of[6], (CH,), 0.5, 3.0, (), jnp.float32),
    }


def lateral(source_field):
    right_side = jnp.pad(source_field[:, :, 1:], ((0, 0), (0, 0), (0, 1)))
    left_side = jnp.pad(source_field[:, :, :-1], ((0, 0), (0, 0), (1, 0)))
    return right_side + left_side


def apply_band(source_field):
    above = jnp.roll(source_field, 1, axis=1)
    below = jnp.roll(source_field, -1, axis=1)
    return -0.25 * (above + below + lateral(source_field))


def chebyshev(source_field):
    collected = [source_field]
    earlier = source_field
    current = source_field
    for degree in range(1, ORDER):
        mapped = apply_band(current)
        if degree == 1:
            following = mapped
        else:
            following = 2.0 * mapped - earlier
        earlier = current
        current = following
        collected.append(following)
    return jnp.stack([member.astype(jnp.bfloat16) for member in collected])


def reference(density, kernel_table, shell_row, theta_first, bias_first, theta_second, bias_second):
    weights = kernel_table[shell_row].astype(jnp.bfloat16)
    weights = lax.optimization_barrier(weights).astype(jnp.float32)

    def add_shell(running, members):
        shell_weight, shell_map = members
        return running + shell_weight[:, None, None] * shell_map.astype(jnp.float32)[None], None

    convergence, _ = lax.scan(add_shell, jnp.zeros((BINS, ROWS, C), jnp.float32), (weights, density))
    first_basis = chebyshev(convergence)
    hidden = jnp.einsum("kbo,kbyx->oyx", theta_first.astype(jnp.float32), first_basis.astype(jnp.float32),
                        precision=lax.Precision.HIGHEST)
    hidden = jnp.maximum(hidden + bias_first[:, None, None], 0.0).astype(jnp.bfloat16)
    group_size = 8
    split_hidden = hidden.reshape(CH // group_size, group_size, ROWS, C)
    split_theta = jnp.transpose(theta_second.reshape(ORDER, CH // group_size, group_size, CH), (1, 0, 2, 3))

    def add_group(running, members):
        group_hidden, group_theta = members
        group_basis = chebyshev(group_hidden.astype(jnp.float32))
        contribution = jnp.einsum("kio,kiyx->oyx", group_theta.astype(jnp.float32), group_basis.astype(jnp.float32),
                                  precision=lax.Precision.HIGHEST)
        return running + contribution, None

    features, _ = lax.scan(add_group, jnp.zeros((CH, ROWS, C), jnp.float32), (split_hidden, split_theta))
    return (features + bias_second[:, None, None]).astype(jnp.bfloat16)
```

```python
import functools

import jax
import jax.numpy as jnp
from jax import lax
from jax.experimental import pallas as pl
from jax.experimental.pallas import tpu as pltpu
from jax.sharding import PartitionSpec as P

MESH = pl.DeviceIdType.MESH
EDGE = 16


def exchange_kernel(
    groups, tiles, density_hbm, table_ref, row_ref, ext_ref,
    dens, part, own, got, load_sem, rs_send, rs_recv, ag_send, ag_recv, up_send, up_recv, dn_send, dn_recv,
):
    me = lax.axis_index("shell")
    tile = lax.axis_index("sky")
    above = lax.rem(tile + tiles - 1, tiles)
    below = lax.rem(tile + 1, tiles)
    shells, rows, width = dens.shape
    bins = part.shape[0]
    load = pltpu.make_async_copy(density_hbm, dens, load_sem)
    load.start()
    barrier = pltpu.get_barrier_semaphore()
    for step in range(1, groups):
        pl.semaphore_signal(barrier, inc=1, device_id=(lax.rem(me + step, groups), tile), device_id_type=MESH)
    for group in range(groups):
        pl.semaphore_signal(barrier, inc=1, device_id=(group, above), device_id_type=MESH)
        pl.semaphore_signal(barrier, inc=1, device_id=(group, below), device_id_type=MESH)
    load.wait()

    def rounded(shell, b):
        weight = table_ref[row_ref[shell], b]
        return jnp.full((8, width), weight, jnp.float32).astype(jnp.bfloat16).astype(jnp.float32)

    block = 16

    def chunk(index, _):
        start = pl.multiple_of(index * block, block)
        sums = [jnp.zeros((block // 8, 8, width), jnp.float32) for _ in range(bins)]

        def add(shell, sums):
            field = dens[shell, pl.ds(start, block), :].astype(jnp.float32).reshape(block // 8, 8, width)
            return tuple(sums[b] + rounded(shell, b)[None] * field for b in range(bins))

        sums = lax.fori_loop(0, shells, add, tuple(sums), unroll=5 if shells % 5 == 0 else 1)
        for b in range(bins):
            total = sums[b].reshape(block, width)
            own[b, pl.ds(start, block), :] = total
            part[b, pl.ds(start, block), :] = total.astype(jnp.bfloat16)
        return 0

    lax.fori_loop(0, rows // block, chunk, 0)
    pl.semaphore_wait(barrier, groups - 1 + 2 * groups)

    reduce_copies = []
    for step in range(1, groups):
        peer = lax.rem(me + step, groups)
        copy = pltpu.make_async_remote_copy(
            src_ref=part.at[peer], dst_ref=got.at[step - 1],
            send_sem=rs_send.at[step - 1], recv_sem=rs_recv.at[step - 1],
            device_id=(peer, tile), device_id_type=MESH)
        copy.start()
        reduce_copies.append(copy)
    for copy in reduce_copies:
        copy.wait_recv()
    total = own[me]
    for step in range(groups - 1):
        total = total + got[step].astype(jnp.float32)
    ext_ref[me, EDGE:EDGE + rows, :] = total.astype(jnp.bfloat16)

    copies = []
    for step in range(1, groups):
        peer = lax.rem(me + step, groups)
        copies.append(pltpu.make_async_remote_copy(
            src_ref=ext_ref.at[me, pl.ds(EDGE, rows)], dst_ref=ext_ref.at[me, pl.ds(EDGE, rows)],
            send_sem=ag_send.at[step - 1], recv_sem=ag_recv.at[me],
            device_id=(peer, tile), device_id_type=MESH))
    for step in range(groups):
        peer = lax.rem(me + step, groups)
        copies.append(pltpu.make_async_remote_copy(
            src_ref=ext_ref.at[me, pl.ds(EDGE, EDGE)], dst_ref=ext_ref.at[me, pl.ds(EDGE + rows, EDGE)],
            send_sem=up_send.at[step], recv_sem=up_recv.at[me],
            device_id=(peer, above), device_id_type=MESH))
        copies.append(pltpu.make_async_remote_copy(
            src_ref=ext_ref.at[me, pl.ds(rows, EDGE)], dst_ref=ext_ref.at[me, pl.ds(0, EDGE)],
            send_sem=dn_send.at[step], recv_sem=dn_recv.at[me],
            device_id=(peer, below), device_id_type=MESH))
    for copy in copies:
        copy.start()
    for step in range(groups):
        peer = lax.rem(me + step, groups)
        if step > 0:
            pltpu.make_async_remote_copy(
                src_ref=ext_ref.at[peer, pl.ds(EDGE, rows)], dst_ref=ext_ref.at[peer, pl.ds(EDGE, rows)],
                send_sem=ag_send.at[step - 1], recv_sem=ag_recv.at[peer],
                device_id=(peer, tile), device_id_type=MESH).wait_recv()
        pltpu.make_async_remote_copy(
            src_ref=ext_ref.at[peer, pl.ds(EDGE, EDGE)], dst_ref=ext_ref.at[peer, pl.ds(EDGE + rows, EDGE)],
            send_sem=up_send.at[step], recv_sem=up_recv.at[peer],
            device_id=(peer, below), device_id_type=MESH).wait_recv()
        pltpu.make_async_remote_copy(
            src_ref=ext_ref.at[peer, pl.ds(rows, EDGE)], dst_ref=ext_ref.at[peer, pl.ds(0, EDGE)],
            send_sem=dn_send.at[step], recv_sem=dn_recv.at[peer],
            device_id=(peer, above), device_id_type=MESH).wait_recv()
    for copy in reduce_copies + copies:
        copy.wait_send()


def exchange(density, kernel_table, shell_row):
    groups = lax.axis_size("shell")
    tiles = lax.axis_size("sky")
    shells, rows, width = density.shape
    bins = kernel_table.shape[1]
    dma = pltpu.SemaphoreType.DMA
    return pl.pallas_call(
        functools.partial(exchange_kernel, groups, tiles),
        out_shape=jax.ShapeDtypeStruct((bins, rows + 2 * EDGE, width), jnp.bfloat16),
        in_specs=[
            pl.BlockSpec(memory_space=pl.ANY),
            pl.BlockSpec(memory_space=pltpu.SMEM),
            pl.BlockSpec(memory_space=pltpu.SMEM),
        ],
        out_specs=pl.BlockSpec(memory_space=pltpu.VMEM),
        scratch_shapes=[
            pltpu.VMEM((shells, rows, width), jnp.bfloat16),
            pltpu.VMEM((bins, rows, width), jnp.bfloat16),
            pltpu.VMEM((bins, rows, width), jnp.float32),
            pltpu.VMEM((groups - 1, rows, width), jnp.bfloat16),
            dma, dma((groups - 1,)), dma((groups - 1,)), dma((groups - 1,)), dma((groups,)),
            dma((groups,)), dma((groups,)), dma((groups,)), dma((groups,)),
        ],
        compiler_params=pltpu.CompilerParams(
            collective_id=0, has_side_effects=True, vmem_limit_bytes=16 * 2**20),
        cost_estimate=pl.CostEstimate(flops=2 * shells * bins * rows * width, bytes_accessed=2 * density.size, transcendentals=0),
    )(density, kernel_table, shell_row)


def conv_kernel(degrees, ext_ref, w1_ref, w2_ref, bias_ref, out_ref, basis, mixed, result):
    bins, span, width = ext_ref.shape
    outs, rows, _ = out_ref.shape
    half = rows // 2
    reach = degrees - 1
    need = half + 2 * reach
    lead = EDGE - 2 * reach
    base = EDGE - reach
    lane8 = lax.broadcasted_iota(jnp.int32, (8, width), 1)

    def lateral(field):
        flat = field.reshape(-1, width)
        lane = lax.broadcasted_iota(jnp.int32, flat.shape, 1)
        right = jnp.where(lane == width - 1, 0.0, pltpu.roll(flat, width - 1, 1))
        left = jnp.where(lane == 0, 0.0, pltpu.roll(flat, 1, 1))
        return (right + left).reshape(field.shape)

    for start in range(0, half + 2 * EDGE, 8):
        pieces = []
        for h in range(2):
            for b in range(bins):
                first = h * half + start
                low = first // 16 * 16
                tall = ext_ref[b, low:low + 16, :].astype(jnp.float32)
                pieces.append(tall[first - low:first - low + 8])
        basis[0, start:start + 8] = jnp.swapaxes(jnp.stack(pieces), 0, 1)

    step = 2
    for k in range(1, degrees):
        first = lead + k
        last = first + half + 4 * reach - 2 * k
        for r in range(first, last, step):
            n = min(step, last - r)
            total = basis[k - 1, r - 1:r - 1 + n] + basis[k - 1, r + 1:r + 1 + n] + lateral(basis[k - 1, r:r + n])
            if k == 1:
                basis[k, r:r + n] = -0.25 * total
            else:
                basis[k, r:r + n] = -0.5 * total - basis[k - 2, r:r + n]

    ones = jnp.ones((16, width), jnp.float32)
    w1 = w1_ref[...]
    w2 = w2_ref[...]
    deep = w2.shape[0] // degrees

    def mix(pair, _):
        columns = []
        for q in range(2):
            row = base + 2 * pair + q
            columns.append(jnp.concatenate([basis[k, row] for k in range(degrees)] + [ones], axis=0))
        operand = jnp.concatenate(columns, axis=1).astype(jnp.bfloat16)
        hidden = jnp.dot(w1, operand, preferred_element_type=jnp.float32)
        hidden = jnp.maximum(hidden, 0.0).astype(jnp.bfloat16)
        u = jnp.dot(w2, hidden, preferred_element_type=jnp.float32)
        for q in range(2):
            for k in range(degrees):
                mixed[k, 2 * pair + q] = u[k * deep:(k + 1) * deep, q * width:(q + 1) * width]
        return 0

    lax.fori_loop(0, need // 2, mix, 0)

    for k in range(degrees - 2, 0, -1):
        first = degrees - 1 - k

        def clenshaw(i, _, k=k, first=first):
            r = first + i
            total = mixed[k + 1, r - 1] + mixed[k + 1, r + 1] + lateral(mixed[k + 1, r])
            value = mixed[k, r] - 0.5 * total
            if k + 2 < degrees:
                value = value - mixed[k + 2, r]
            mixed[k, r] = value
            return 0

        lax.fori_loop(0, need - 2 * first, clenshaw, 0, unroll=2)

    def finish(block, _):
        values = []
        for i in range(8):
            r = reach + block * 8 + i
            total = mixed[1, r - 1] + mixed[1, r + 1] + lateral(mixed[1, r])
            values.append(mixed[0, r] - 0.25 * total - mixed[2, r])
        stacked = jnp.stack(values)
        for h in range(2):
            start = pl.multiple_of(h * half + block * 8, 8)
            result[:, pl.ds(start, 8), :] = jnp.swapaxes(stacked[:, h * outs:(h + 1) * outs], 0, 1)
        return 0

    lax.fori_loop(0, half // 8, finish, 0)
    shell = lax.axis_index("shell")
    for o in range(outs):
        out_ref[o] = (result[o] + bias_ref[shell * outs + o]).astype(jnp.bfloat16)


def three_parts(values):
    high = lax.reduce_precision(values, 8, 7)
    rest = values - high
    mid = lax.reduce_precision(rest, 8, 7)
    return jnp.stack([high, mid, rest - mid])


def per_device(
    density, kernel_table, shell_row, theta_first, bias_first, theta_second, bias_second
):
    degrees, bins, channels = theta_first.shape
    groups = lax.axis_size("shell")
    shell = lax.axis_index("shell")
    rows, width = density.shape[1:]
    outs = theta_second.shape[2] // groups

    eye = jnp.eye(2, dtype=jnp.bfloat16)
    w1 = jnp.einsum("kbo,hg->hokgb", theta_first, eye).reshape(2 * channels, degrees * 2 * bins)
    bias_cols = three_parts(bias_first).astype(jnp.bfloat16).T
    bias_cols = jnp.pad(jnp.concatenate([bias_cols, bias_cols]), ((0, 0), (0, 13)))
    w1 = jnp.concatenate([w1, bias_cols], axis=1)
    cols = lax.dynamic_slice_in_dim(theta_second, shell * outs, outs, 2)
    w2 = jnp.einsum("kio,hg->khogi", cols, eye).reshape(degrees * 2 * outs, 2 * channels)

    ext = exchange(density, kernel_table, shell_row)
    half = rows // 2
    need = half + 2 * (degrees - 1)
    vmem = pl.BlockSpec(memory_space=pltpu.VMEM)
    return pl.pallas_call(
        functools.partial(conv_kernel, degrees),
        out_shape=jax.ShapeDtypeStruct((outs, rows, width), jnp.bfloat16),
        in_specs=[vmem, vmem, vmem, pl.BlockSpec(memory_space=pltpu.SMEM)],
        out_specs=vmem,
        scratch_shapes=[
            pltpu.VMEM((degrees, half + 2 * EDGE, 2 * bins, width), jnp.float32),
            pltpu.VMEM((degrees, need, 2 * outs, width), jnp.float32),
            pltpu.VMEM((outs, rows, width), jnp.float32),
        ],
        compiler_params=pltpu.CompilerParams(vmem_limit_bytes=40 * 2**20),
    )(ext, w1, w2, bias_second)


def solution(mesh):
    return jax.shard_map(
        per_device,
        mesh=mesh,
        in_specs=(P("shell", "sky", None), P(), P("shell"), P(), P(), P(), P()),
        out_specs=P("shell", "sky", None),
        check_vma=False,
    )
```

```python
import functools

import jax
import jax.numpy as jnp
from jax import lax
from jax.experimental import pallas as pl
from jax.experimental.pallas import tpu as pltpu
from jax.sharding import PartitionSpec as P

MESH = pl.DeviceIdType.MESH
EDGE = 16
CL = 1
MIXU = True


def exchange_kernel(
    groups, tiles, density_hbm, table_ref, row_ref, ext_ref,
    dens, part, own, got, load_sem, rs_send, rs_recv, ag_send, ag_recv, up_send, up_recv, dn_send, dn_recv,
):
    me = lax.axis_index("shell")
    tile = lax.axis_index("sky")
    above = lax.rem(tile + tiles - 1, tiles)
    below = lax.rem(tile + 1, tiles)
    shells, rows, width = dens.shape
    bins = part.shape[0]
    load = pltpu.make_async_copy(density_hbm, dens, load_sem)
    load.start()
    barrier = pltpu.get_barrier_semaphore()
    for step in range(1, groups):
        pl.semaphore_signal(barrier, inc=1, device_id=(lax.rem(me + step, groups), tile), device_id_type=MESH)
    for group in range(groups):
        pl.semaphore_signal(barrier, inc=1, device_id=(group, above), device_id_type=MESH)
        pl.semaphore_signal(barrier, inc=1, device_id=(group, below), device_id_type=MESH)
    load.wait()

    block = EDGE
    chunks = rows // block
    order = [0, chunks - 1] + list(range(1, chunks - 1))
    per_trip = 5 if shells % 5 == 0 else 1
    started = []
    for turn, c in enumerate(order):
        span = pl.ds(c * block, block)

        def add(shell, sums):
            field = dens[shell, c * block:(c + 1) * block, :].astype(jnp.float32)
            return tuple(sums[b] + table_ref[row_ref[shell], b] * field for b in range(bins))

        sums = tuple(jnp.zeros((block, width), jnp.float32) for _ in range(bins))
        sums = lax.fori_loop(0, shells, add, sums, unroll=per_trip)
        for b in range(bins):
            own[b, c * block:(c + 1) * block, :] = sums[b]
            part[b, c * block:(c + 1) * block, :] = sums[b].astype(jnp.bfloat16)
        if turn == 0:
            pl.semaphore_wait(barrier, groups - 1 + 2 * groups)
        for step in range(1, groups):
            peer = lax.rem(me + step, groups)
            copy = pltpu.make_async_remote_copy(
                src_ref=part.at[peer, span], dst_ref=got.at[step - 1, span],
                send_sem=rs_send.at[step - 1, c], recv_sem=rs_recv.at[step - 1, c],
                device_id=(peer, tile), device_id_type=MESH)
            copy.start()
            started.append(copy)

    def gather_copy(owner, peer, c, sem):
        place = ext_ref.at[owner, pl.ds(EDGE + c * block, block)]
        return pltpu.make_async_remote_copy(
            src_ref=place, dst_ref=place, send_sem=ag_send.at[sem, c], recv_sem=ag_recv.at[owner, c],
            device_id=(peer, tile), device_id_type=MESH)

    def up_copy(owner, peer, beside, sem):
        return pltpu.make_async_remote_copy(
            src_ref=ext_ref.at[owner, pl.ds(EDGE, EDGE)], dst_ref=ext_ref.at[owner, pl.ds(EDGE + rows, EDGE)],
            send_sem=up_send.at[sem], recv_sem=up_recv.at[owner],
            device_id=(peer, beside), device_id_type=MESH)

    def down_copy(owner, peer, beside, sem):
        return pltpu.make_async_remote_copy(
            src_ref=ext_ref.at[owner, pl.ds(rows, EDGE)], dst_ref=ext_ref.at[owner, pl.ds(0, EDGE)],
            send_sem=dn_send.at[sem], recv_sem=dn_recv.at[owner],
            device_id=(peer, beside), device_id_type=MESH)

    for turn, c in enumerate(order):
        for step in range(1, groups):
            started[turn * (groups - 1) + step - 1].wait_recv()
        total = own[me, c * block:(c + 1) * block, :]
        for step in range(groups - 1):
            total = total + got[step, c * block:(c + 1) * block, :].astype(jnp.float32)
        ext_ref[me, EDGE + c * block:EDGE + (c + 1) * block, :] = total.astype(jnp.bfloat16)
        for step in range(groups - 1, -1, -1):
            peer = lax.rem(me + step, groups)
            if step > 0:
                copy = gather_copy(me, peer, c, step - 1)
                copy.start()
                started.append(copy)
            if c == 0:
                copy = up_copy(me, peer, above, step)
                copy.start()
                started.append(copy)
            if c == chunks - 1:
                copy = down_copy(me, peer, below, step)
                copy.start()
                started.append(copy)
    for step in range(groups):
        peer = lax.rem(me + step, groups)
        if step > 0:
            for c in range(chunks):
                gather_copy(peer, peer, c, step - 1).wait_recv()
        up_copy(peer, peer, below, step).wait_recv()
        down_copy(peer, peer, above, step).wait_recv()
    for copy in started:
        copy.wait_send()


def exchange(density, kernel_table, shell_row):
    groups = lax.axis_size("shell")
    tiles = lax.axis_size("sky")
    shells, rows, width = density.shape
    bins = kernel_table.shape[1]
    dma = pltpu.SemaphoreType.DMA
    chunks = rows // EDGE
    return pl.pallas_call(
        functools.partial(exchange_kernel, groups, tiles),
        out_shape=jax.ShapeDtypeStruct((bins, rows + 2 * EDGE, width), jnp.bfloat16),
        in_specs=[
            pl.BlockSpec(memory_space=pl.ANY),
            pl.BlockSpec(memory_space=pltpu.SMEM),
            pl.BlockSpec(memory_space=pltpu.SMEM),
        ],
        out_specs=pl.BlockSpec(memory_space=pltpu.VMEM),
        scratch_shapes=[
            pltpu.VMEM((shells, rows, width), jnp.bfloat16),
            pltpu.VMEM((bins, rows, width), jnp.bfloat16),
            pltpu.VMEM((bins, rows, width), jnp.float32),
            pltpu.VMEM((groups - 1, rows, width), jnp.bfloat16),
            dma, dma((groups - 1, chunks)), dma((groups - 1, chunks)), dma((groups - 1, chunks)), dma((groups, chunks)),
            dma((groups,)), dma((groups,)), dma((groups,)), dma((groups,)),
        ],
        compiler_params=pltpu.CompilerParams(
            collective_id=0, has_side_effects=True, vmem_limit_bytes=56 * 2**20),
        cost_estimate=pl.CostEstimate(flops=2 * shells * bins * rows * width, bytes_accessed=2 * density.size, transcendentals=0),
    )(density, lax.reduce_precision(kernel_table, 8, 7), shell_row)


def conv_kernel(degrees, ext_ref, w1_ref, w2_ref, bias_ref, out_ref, basis, mixed, result):
    bins, span, width = ext_ref.shape
    outs, rows, _ = out_ref.shape
    half = rows // 2
    reach = degrees - 1
    need = half + 2 * reach
    lead = EDGE - 2 * reach
    base = EDGE - reach

    def lateral(field):
        flat = field.reshape(-1, width)
        lane = lax.broadcasted_iota(jnp.int32, flat.shape, 1)
        right = jnp.where(lane == width - 1, 0.0, pltpu.roll(flat, width - 1, 1))
        left = jnp.where(lane == 0, 0.0, pltpu.roll(flat, 1, 1))
        return (right + left).reshape(field.shape)

    for start in range(0, half + 2 * EDGE, 8):
        pieces = []
        for h in range(2):
            for b in range(bins):
                first = h * half + start
                low = first // 16 * 16
                tall = ext_ref[b, low:low + 16, :].astype(jnp.float32)
                pieces.append(tall[first - low:first - low + 8])
        basis[0, start:start + 8] = jnp.swapaxes(jnp.stack(pieces), 0, 1)

    step = 2
    for k in range(1, degrees):
        first = lead + k
        last = first + half + 4 * reach - 2 * k
        for r in range(first, last, step):
            n = min(step, last - r)
            total = basis[k - 1, r - 1:r - 1 + n] + basis[k - 1, r + 1:r + 1 + n] + lateral(basis[k - 1, r:r + n])
            if k == 1:
                basis[k, r:r + n] = -0.25 * total
            else:
                basis[k, r:r + n] = -0.5 * total - basis[k - 2, r:r + n]

    ones = jnp.ones((16, width), jnp.float32)
    w1 = w1_ref[...]
    w2 = w2_ref[...]
    deep = w2.shape[0] // degrees

    def mix(pair, _):
        columns = []
        for q in range(2):
            row = base + 2 * pair + q
            columns.append(jnp.concatenate([basis[k, row] for k in range(degrees)] + [ones], axis=0))
        operand = jnp.concatenate(columns, axis=1).astype(jnp.bfloat16)
        hidden = jnp.dot(w1, operand, preferred_element_type=jnp.float32)
        hidden = jnp.maximum(hidden, 0.0).astype(jnp.bfloat16)
        u = jnp.dot(w2, hidden, preferred_element_type=jnp.float32)
        for q in range(2):
            for k in range(degrees):
                mixed[k, 2 * pair + q] = u[k * deep:(k + 1) * deep, q * width:(q + 1) * width]
        return 0

    lax.fori_loop(0, need // 2, mix, 0, unroll=MIXU)

    for k in range(degrees - 2, 0, -1):
        first = degrees - 1 - k

        def clenshaw(r, n, k=k):
            value = mixed[k, pl.ds(r, n)] - 0.5 * (
                mixed[k + 1, pl.ds(r - 1, n)] + mixed[k + 1, pl.ds(r + 1, n)] + lateral(mixed[k + 1, pl.ds(r, n)]))
            if k + 2 < degrees:
                value = value - mixed[k + 2, pl.ds(r, n)]
            mixed[k, pl.ds(r, n)] = value

        count = need - 2 * first
        for i in range(count // CL):
            clenshaw(first + i * CL, CL)
        if count % CL:
            clenshaw(first + count // CL * CL, count % CL)

    def finish(block, _):
        values = []
        for i in range(8):
            r = reach + block * 8 + i
            total = mixed[1, r - 1] + mixed[1, r + 1] + lateral(mixed[1, r])
            values.append(mixed[0, r] - 0.25 * total - mixed[2, r])
        stacked = jnp.stack(values)
        for h in range(2):
            start = pl.multiple_of(h * half + block * 8, 8)
            result[:, pl.ds(start, 8), :] = jnp.swapaxes(stacked[:, h * outs:(h + 1) * outs], 0, 1)
        return 0

    lax.fori_loop(0, half // 8, finish, 0)
    shell = lax.axis_index("shell")
    for o in range(outs):
        out_ref[o] = (result[o] + bias_ref[shell * outs + o]).astype(jnp.bfloat16)


def three_parts(values):
    high = lax.reduce_precision(values, 8, 7)
    rest = values - high
    mid = lax.reduce_precision(rest, 8, 7)
    return jnp.stack([high, mid, rest - mid])


def per_device(
    density, kernel_table, shell_row, theta_first, bias_first, theta_second, bias_second
):
    degrees, bins, channels = theta_first.shape
    groups = lax.axis_size("shell")
    shell = lax.axis_index("shell")
    rows, width = density.shape[1:]
    outs = theta_second.shape[2] // groups

    eye = jnp.eye(2, dtype=jnp.bfloat16)
    w1 = jnp.einsum("kbo,hg->hokgb", theta_first, eye).reshape(2 * channels, degrees * 2 * bins)
    bias_cols = three_parts(bias_first).astype(jnp.bfloat16).T
    bias_cols = jnp.pad(jnp.concatenate([bias_cols, bias_cols]), ((0, 0), (0, 13)))
    w1 = jnp.concatenate([w1, bias_cols], axis=1)
    cols = lax.dynamic_slice_in_dim(theta_second, shell * outs, outs, 2)
    w2 = jnp.einsum("kio,hg->khogi", cols, eye).reshape(degrees * 2 * outs, 2 * channels)

    ext = exchange(density, kernel_table, shell_row)
    half = rows // 2
    need = half + 2 * (degrees - 1)
    vmem = pl.BlockSpec(memory_space=pltpu.VMEM)
    return pl.pallas_call(
        functools.partial(conv_kernel, degrees),
        out_shape=jax.ShapeDtypeStruct((outs, rows, width), jnp.bfloat16),
        in_specs=[vmem, vmem, vmem, pl.BlockSpec(memory_space=pltpu.SMEM)],
        out_specs=vmem,
        scratch_shapes=[
            pltpu.VMEM((degrees, half + 2 * EDGE, 2 * bins, width), jnp.float32),
            pltpu.VMEM((degrees, need, 2 * outs, width), jnp.float32),
            pltpu.VMEM((outs, rows, width), jnp.float32),
        ],
        compiler_params=pltpu.CompilerParams(vmem_limit_bytes=40 * 2**20),
    )(ext, w1, w2, bias_second)


def solution(mesh):
    return jax.shard_map(
        per_device,
        mesh=mesh,
        in_specs=(P("shell", "sky", None), P(), P("shell"), P(), P(), P(), P()),
        out_specs=P("shell", "sky", None),
        check_vma=False,
    )
```

```python
import functools

import jax
import jax.numpy as jnp
from jax import lax
from jax.experimental import pallas as pl
from jax.experimental.pallas import tpu as pltpu
from jax.sharding import PartitionSpec as P

MESH = pl.DeviceIdType.MESH
EDGE = 16
CL = 1
MIXU = True


def exchange_kernel(
    groups, tiles, density_hbm, table_ref, row_ref, ext_ref,
    dens, weights, part, own, got, load_sem, rs_send, rs_recv, ag_send, ag_recv, up_send, up_recv, dn_send, dn_recv,
):
    me = lax.axis_index("shell")
    tile = lax.axis_index("sky")
    above = lax.rem(tile + tiles - 1, tiles)
    below = lax.rem(tile + 1, tiles)
    shells, rows, width = dens.shape
    bins = part.shape[0]
    load = pltpu.make_async_copy(density_hbm, dens, load_sem)
    load.start()
    barrier = pltpu.get_barrier_semaphore()
    for step in range(1, groups):
        pl.semaphore_signal(barrier, inc=1, device_id=(lax.rem(me + step, groups), tile), device_id_type=MESH)
    for group in range(groups):
        pl.semaphore_signal(barrier, inc=1, device_id=(group, above), device_id_type=MESH)
        pl.semaphore_signal(barrier, inc=1, device_id=(group, below), device_id_type=MESH)
    for b in range(bins):
        for shell in range(shells):
            weight = jnp.full((EDGE, 128), table_ref[b, row_ref[shell]], jnp.float32)
            weights[shell, b] = weight.astype(jnp.bfloat16).astype(jnp.float32)[:8]
    load.wait()

    block = EDGE
    chunks = rows // block
    order = [0, chunks - 1] + list(range(1, chunks - 1))
    per_trip = 5 if shells % 5 == 0 else 1
    started = []
    for turn, c in enumerate(order):
        span = pl.ds(c * block, block)

        def add(shell, sums):
            field = dens[shell, c * block:(c + 1) * block, :].astype(jnp.float32)
            wide = [jnp.tile(weights[shell, b], (block // 8, width // 128)) for b in range(bins)]
            return tuple(sums[b] + wide[b] * field for b in range(bins))

        sums = tuple(jnp.zeros((block, width), jnp.float32) for _ in range(bins))
        sums = lax.fori_loop(0, shells, add, sums, unroll=per_trip)
        for b in range(bins):
            own[b, c * block:(c + 1) * block, :] = sums[b]
            part[b, c * block:(c + 1) * block, :] = sums[b].astype(jnp.bfloat16)
        if turn == 0:
            pl.semaphore_wait(barrier, groups - 1 + 2 * groups)
        for step in range(1, groups):
            peer = lax.rem(me + step, groups)
            copy = pltpu.make_async_remote_copy(
                src_ref=part.at[peer, span], dst_ref=got.at[step - 1, span],
                send_sem=rs_send.at[step - 1, c], recv_sem=rs_recv.at[step - 1, c],
                device_id=(peer, tile), device_id_type=MESH)
            copy.start()
            started.append(copy)

    def gather_copy(owner, peer, c, sem):
        place = ext_ref.at[owner, pl.ds(EDGE + c * block, block)]
        return pltpu.make_async_remote_copy(
            src_ref=place, dst_ref=place, send_sem=ag_send.at[sem, c], recv_sem=ag_recv.at[owner, c],
            device_id=(peer, tile), device_id_type=MESH)

    def up_copy(owner, peer, beside, sem):
        return pltpu.make_async_remote_copy(
            src_ref=ext_ref.at[owner, pl.ds(EDGE, EDGE)], dst_ref=ext_ref.at[owner, pl.ds(EDGE + rows, EDGE)],
            send_sem=up_send.at[sem], recv_sem=up_recv.at[owner],
            device_id=(peer, beside), device_id_type=MESH)

    def down_copy(owner, peer, beside, sem):
        return pltpu.make_async_remote_copy(
            src_ref=ext_ref.at[owner, pl.ds(rows, EDGE)], dst_ref=ext_ref.at[owner, pl.ds(0, EDGE)],
            send_sem=dn_send.at[sem], recv_sem=dn_recv.at[owner],
            device_id=(peer, beside), device_id_type=MESH)

    for turn, c in enumerate(order):
        for step in range(1, groups):
            started[turn * (groups - 1) + step - 1].wait_recv()
        total = own[me, c * block:(c + 1) * block, :]
        for step in range(groups - 1):
            total = total + got[step, c * block:(c + 1) * block, :].astype(jnp.float32)
        ext_ref[me, EDGE + c * block:EDGE + (c + 1) * block, :] = total.astype(jnp.bfloat16)
        for step in range(groups - 1, -1, -1):
            peer = lax.rem(me + step, groups)
            if step > 0:
                copy = gather_copy(me, peer, c, step - 1)
                copy.start()
                started.append(copy)
            if c == 0:
                copy = up_copy(me, peer, above, step)
                copy.start()
                started.append(copy)
            if c == chunks - 1:
                copy = down_copy(me, peer, below, step)
                copy.start()
                started.append(copy)
    for step in range(groups):
        peer = lax.rem(me + step, groups)
        if step > 0:
            for c in range(chunks):
                gather_copy(peer, peer, c, step - 1).wait_recv()
        up_copy(peer, peer, below, step).wait_recv()
        down_copy(peer, peer, above, step).wait_recv()
    for copy in started:
        copy.wait_send()


def exchange(density, kernel_table, shell_row):
    groups = lax.axis_size("shell")
    tiles = lax.axis_size("sky")
    shells, rows, width = density.shape
    bins = kernel_table.shape[1]
    dma = pltpu.SemaphoreType.DMA
    chunks = rows // EDGE
    return pl.pallas_call(
        functools.partial(exchange_kernel, groups, tiles),
        out_shape=jax.ShapeDtypeStruct((bins, rows + 2 * EDGE, width), jnp.bfloat16),
        in_specs=[
            pl.BlockSpec(memory_space=pl.ANY),
            pl.BlockSpec(memory_space=pltpu.SMEM),
            pl.BlockSpec(memory_space=pltpu.SMEM),
        ],
        out_specs=pl.BlockSpec(memory_space=pltpu.VMEM),
        scratch_shapes=[
            pltpu.VMEM((shells, rows, width), jnp.bfloat16),
            pltpu.VMEM((shells, bins, 8, 128), jnp.float32),
            pltpu.VMEM((bins, rows, width), jnp.bfloat16),
            pltpu.VMEM((bins, rows, width), jnp.float32),
            pltpu.VMEM((groups - 1, rows, width), jnp.bfloat16),
            dma, dma((groups - 1, chunks)), dma((groups - 1, chunks)), dma((groups - 1, chunks)), dma((groups, chunks)),
            dma((groups,)), dma((groups,)), dma((groups,)), dma((groups,)),
        ],
        compiler_params=pltpu.CompilerParams(
            collective_id=0, has_side_effects=True, vmem_limit_bytes=58 * 2**20),
        cost_estimate=pl.CostEstimate(flops=2 * shells * bins * rows * width, bytes_accessed=2 * density.size, transcendentals=0),
    )(density, kernel_table.T, shell_row)


def conv_kernel(ext_hbm, first_ref, lift_ref, second_ref, bias_ref, out_ref, ext_ref, basis, mixed, result, flat_first, turned, sem):
    load = pltpu.make_async_copy(ext_hbm, ext_ref, sem)
    load.start()
    degrees, bins, channels = first_ref.shape
    width = ext_ref.shape[2]
    shell = lax.axis_index("shell")
    outs, rows, _ = out_ref.shape
    half = rows // 2
    reach = degrees - 1
    need = half + 2 * reach
    lead = EDGE - 2 * reach
    base = EDGE - reach

    flat_first[...] = jnp.zeros_like(flat_first)
    for h in range(2):
        span = slice(h * channels, (h + 1) * channels)
        for k in range(degrees):
            row = (2 * k + h) * bins
            flat_first[row:row + bins, span] = first_ref[k].astype(jnp.float32)
        rest = lift_ref[...]
        for part in range(3):
            row = 2 * bins * degrees + part
            high = rest.astype(jnp.bfloat16).astype(jnp.float32)
            flat_first[row:row + 1, span] = high
            rest = rest - high
    w1 = flat_first[...].T.astype(jnp.bfloat16)
    lanes = lax.broadcasted_iota(jnp.int32, (outs, 2 * channels), 1)
    pieces = []
    for k in range(degrees):
        across = second_ref[k].astype(jnp.float32).T
        turned[k] = jnp.concatenate([across, across], axis=1)
        mine = turned[k, pl.ds(pl.multiple_of(shell * outs, outs), outs), :]
        pieces.append(jnp.where(lanes < channels, mine, 0.0))
        pieces.append(jnp.where(lanes < channels, 0.0, mine))
    w2 = jnp.concatenate(pieces, axis=0).astype(jnp.bfloat16)
    load.wait()

    def lateral(field):
        flat = field.reshape(-1, width)
        lane = lax.broadcasted_iota(jnp.int32, flat.shape, 1)
        right = jnp.where(lane == width - 1, 0.0, pltpu.roll(flat, width - 1, 1))
        left = jnp.where(lane == 0, 0.0, pltpu.roll(flat, 1, 1))
        return (right + left).reshape(field.shape)

    for start in range(0, half + 2 * EDGE, 8):
        pieces = []
        for h in range(2):
            for b in range(bins):
                first = h * half + start
                low = first // 16 * 16
                tall = ext_ref[b, low:low + 16, :].astype(jnp.float32)
                pieces.append(tall[first - low:first - low + 8])
        basis[0, start:start + 8] = jnp.swapaxes(jnp.stack(pieces), 0, 1)

    step = 2
    for k in range(1, degrees):
        first = lead + k
        last = first + half + 4 * reach - 2 * k
        for r in range(first, last, step):
            n = min(step, last - r)
            total = basis[k - 1, r - 1:r - 1 + n] + basis[k - 1, r + 1:r + 1 + n] + lateral(basis[k - 1, r:r + n])
            if k == 1:
                basis[k, r:r + n] = -0.25 * total
            else:
                basis[k, r:r + n] = -0.5 * total - basis[k - 2, r:r + n]

    ones = jnp.ones((16, width), jnp.float32)
    deep = w2.shape[0] // degrees

    def mix(pair, _):
        columns = []
        for q in range(2):
            row = base + 2 * pair + q
            columns.append(jnp.concatenate([basis[k, row] for k in range(degrees)] + [ones], axis=0))
        operand = jnp.concatenate(columns, axis=1).astype(jnp.bfloat16)
        hidden = jnp.dot(w1, operand, preferred_element_type=jnp.float32)
        hidden = jnp.maximum(hidden, 0.0).astype(jnp.bfloat16)
        u = jnp.dot(w2, hidden, preferred_element_type=jnp.float32)
        for q in range(2):
            for k in range(degrees):
                mixed[k, 2 * pair + q] = u[k * deep:(k + 1) * deep, q * width:(q + 1) * width]
        return 0

    lax.fori_loop(0, need // 2, mix, 0, unroll=MIXU)

    for k in range(degrees - 2, 0, -1):
        first = degrees - 1 - k

        def clenshaw(r, n, k=k):
            value = mixed[k, pl.ds(r, n)] - 0.5 * (
                mixed[k + 1, pl.ds(r - 1, n)] + mixed[k + 1, pl.ds(r + 1, n)] + lateral(mixed[k + 1, pl.ds(r, n)]))
            if k + 2 < degrees:
                value = value - mixed[k + 2, pl.ds(r, n)]
            mixed[k, pl.ds(r, n)] = value

        count = need - 2 * first
        for i in range(count // CL):
            clenshaw(first + i * CL, CL)
        if count % CL:
            clenshaw(first + count // CL * CL, count % CL)

    def finish(block, _):
        values = []
        for i in range(8):
            r = reach + block * 8 + i
            total = mixed[1, r - 1] + mixed[1, r + 1] + lateral(mixed[1, r])
            values.append(mixed[0, r] - 0.25 * total - mixed[2, r])
        stacked = jnp.stack(values)
        for h in range(2):
            start = pl.multiple_of(h * half + block * 8, 8)
            result[:, pl.ds(start, 8), :] = jnp.swapaxes(stacked[:, h * outs:(h + 1) * outs], 0, 1)
        return 0

    lax.fori_loop(0, half // 8, finish, 0)
    for o in range(outs):
        out_ref[o] = (result[o] + bias_ref[shell * outs + o]).astype(jnp.bfloat16)


def per_device(
    density, kernel_table, shell_row, theta_first, bias_first, theta_second, bias_second
):
    degrees, bins, channels = theta_first.shape
    groups = lax.axis_size("shell")
    rows, width = density.shape[1:]
    outs = theta_second.shape[2] // groups
    ext = exchange(density, kernel_table, shell_row)
    half = rows // 2
    need = half + 2 * (degrees - 1)
    vmem = pl.BlockSpec(memory_space=pltpu.VMEM)
    return pl.pallas_call(
        conv_kernel,
        out_shape=jax.ShapeDtypeStruct((outs, rows, width), jnp.bfloat16),
        in_specs=[pl.BlockSpec(memory_space=pl.ANY), vmem, vmem, vmem, pl.BlockSpec(memory_space=pltpu.SMEM)],
        out_specs=vmem,
        scratch_shapes=[
            pltpu.VMEM(ext.shape, ext.dtype),
            pltpu.VMEM((degrees, half + 2 * EDGE, 2 * bins, width), jnp.float32),
            pltpu.VMEM((degrees, need, 2 * outs, width), jnp.float32),
            pltpu.VMEM((outs, rows, width), jnp.float32),
            pltpu.VMEM((2 * bins * degrees + 16, 2 * channels), jnp.float32),
            pltpu.VMEM((degrees, channels, 2 * channels), jnp.float32),
            pltpu.SemaphoreType.DMA,
        ],
        compiler_params=pltpu.CompilerParams(vmem_limit_bytes=58 * 2**20),
    )(ext, theta_first, bias_first.reshape(1, channels), theta_second, bias_second)


def solution(mesh):
    return jax.shard_map(
        per_device,
        mesh=mesh,
        in_specs=(P("shell", "sky", None), P(), P("shell"), P(), P(), P(), P()),
        out_specs=P("shell", "sky", None),
        check_vma=False,
    )
```

```python
import functools

import jax
import jax.numpy as jnp
from jax import lax
from jax.experimental import pallas as pl
from jax.experimental.pallas import tpu as pltpu
from jax.sharding import PartitionSpec as P

MESH = pl.DeviceIdType.MESH
EDGE = 16


def exchange_kernel(
    groups, tiles, density_hbm, table_ref, row_ref, ext_ref,
    dens, weights, part, own, got, load_sem, rs_send, rs_recv, ag_send, ag_recv, up_send, up_recv, dn_send, dn_recv,
):
    me = lax.axis_index("shell")
    tile = lax.axis_index("sky")
    above = lax.rem(tile + tiles - 1, tiles)
    below = lax.rem(tile + 1, tiles)
    shells, rows, width = dens.shape
    bins = part.shape[0]
    load = pltpu.make_async_copy(density_hbm, dens, load_sem)
    load.start()
    barrier = pltpu.get_barrier_semaphore()
    for step in range(1, groups):
        pl.semaphore_signal(barrier, inc=1, device_id=(lax.rem(me + step, groups), tile), device_id_type=MESH)
    for group in range(groups):
        pl.semaphore_signal(barrier, inc=1, device_id=(group, above), device_id_type=MESH)
        pl.semaphore_signal(barrier, inc=1, device_id=(group, below), device_id_type=MESH)
    for b in range(bins):
        for shell in range(shells):
            weight = jnp.full((EDGE, 128), table_ref[b, row_ref[shell]], jnp.float32)
            weights[shell, b] = weight.astype(jnp.bfloat16).astype(jnp.float32)[:8]
    load.wait()

    block = EDGE
    chunks = rows // block
    order = [0, chunks - 1] + list(range(1, chunks - 1))
    per_trip = 5 if shells % 5 == 0 else 1
    started = []
    for turn, c in enumerate(order):
        span = pl.ds(c * block, block)

        def add(shell, sums):
            field = dens[shell, c * block:(c + 1) * block, :].astype(jnp.float32)
            wide = [jnp.tile(weights[shell, b], (block // 8, width // 128)) for b in range(bins)]
            return tuple(sums[b] + wide[b] * field for b in range(bins))

        sums = tuple(jnp.zeros((block, width), jnp.float32) for _ in range(bins))
        sums = lax.fori_loop(0, shells, add, sums, unroll=per_trip)
        for b in range(bins):
            own[b, c * block:(c + 1) * block, :] = sums[b]
            part[b, c * block:(c + 1) * block, :] = sums[b].astype(jnp.bfloat16)
        if turn == 0:
            pl.semaphore_wait(barrier, groups - 1 + 2 * groups)
        for step in range(1, groups):
            peer = lax.rem(me + step, groups)
            copy = pltpu.make_async_remote_copy(
                src_ref=part.at[peer, span], dst_ref=got.at[step - 1, span],
                send_sem=rs_send.at[step - 1, c], recv_sem=rs_recv.at[step - 1, c],
                device_id=(peer, tile), device_id_type=MESH)
            copy.start()
            started.append(copy)

    def gather_copy(owner, peer, c, sem):
        place = ext_ref.at[owner, pl.ds(EDGE + c * block, block)]
        return pltpu.make_async_remote_copy(
            src_ref=place, dst_ref=place, send_sem=ag_send.at[sem, c], recv_sem=ag_recv.at[owner, c],
            device_id=(peer, tile), device_id_type=MESH)

    def up_copy(owner, peer, beside, sem):
        return pltpu.make_async_remote_copy(
            src_ref=ext_ref.at[owner, pl.ds(EDGE, EDGE)], dst_ref=ext_ref.at[owner, pl.ds(EDGE + rows, EDGE)],
            send_sem=up_send.at[sem], recv_sem=up_recv.at[owner],
            device_id=(peer, beside), device_id_type=MESH)

    def down_copy(owner, peer, beside, sem):
        return pltpu.make_async_remote_copy(
            src_ref=ext_ref.at[owner, pl.ds(rows, EDGE)], dst_ref=ext_ref.at[owner, pl.ds(0, EDGE)],
            send_sem=dn_send.at[sem], recv_sem=dn_recv.at[owner],
            device_id=(peer, beside), device_id_type=MESH)

    for turn, c in enumerate(order):
        for step in range(1, groups):
            started[turn * (groups - 1) + step - 1].wait_recv()
        total = own[me, c * block:(c + 1) * block, :]
        for step in range(groups - 1):
            total = total + got[step, c * block:(c + 1) * block, :].astype(jnp.float32)
        ext_ref[me, EDGE + c * block:EDGE + (c + 1) * block, :] = total.astype(jnp.bfloat16)
        for step in range(groups - 1, -1, -1):
            peer = lax.rem(me + step, groups)
            if step > 0:
                copy = gather_copy(me, peer, c, step - 1)
                copy.start()
                started.append(copy)
            if c == 0:
                copy = up_copy(me, peer, above, step)
                copy.start()
                started.append(copy)
            if c == chunks - 1:
                copy = down_copy(me, peer, below, step)
                copy.start()
                started.append(copy)
    for step in range(groups):
        peer = lax.rem(me + step, groups)
        if step > 0:
            for c in range(chunks):
                gather_copy(peer, peer, c, step - 1).wait_recv()
        up_copy(peer, peer, below, step).wait_recv()
        down_copy(peer, peer, above, step).wait_recv()
    for copy in started:
        copy.wait_send()


def exchange(density, kernel_table, shell_row):
    groups = lax.axis_size("shell")
    tiles = lax.axis_size("sky")
    shells, rows, width = density.shape
    bins = kernel_table.shape[1]
    dma = pltpu.SemaphoreType.DMA
    chunks = rows // EDGE
    return pl.pallas_call(
        functools.partial(exchange_kernel, groups, tiles),
        out_shape=pltpu.VMEM((bins, rows + 2 * EDGE, width), jnp.bfloat16),
        in_specs=[
            pl.BlockSpec(memory_space=pl.ANY),
            pl.BlockSpec(memory_space=pltpu.SMEM),
            pl.BlockSpec(memory_space=pltpu.SMEM),
        ],
        out_specs=pl.BlockSpec(memory_space=pltpu.VMEM),
        scratch_shapes=[
            pltpu.VMEM((shells, rows, width), jnp.bfloat16),
            pltpu.VMEM((shells, bins, 8, 128), jnp.float32),
            pltpu.VMEM((bins, rows, width), jnp.bfloat16),
            pltpu.VMEM((bins, rows, width), jnp.float32),
            pltpu.VMEM((groups - 1, rows, width), jnp.bfloat16),
            dma, dma((groups - 1, chunks)), dma((groups - 1, chunks)), dma((groups - 1, chunks)), dma((groups, chunks)),
            dma((groups,)), dma((groups,)), dma((groups,)), dma((groups,)),
        ],
        compiler_params=pltpu.CompilerParams(
            collective_id=0, has_side_effects=True, vmem_limit_bytes=58 * 2**20),
        cost_estimate=pl.CostEstimate(flops=2 * shells * bins * rows * width, bytes_accessed=2 * density.size, transcendentals=0),
    )(density, kernel_table.T, shell_row)


def conv_kernel(ext_ref, first_ref, lift_ref, second_ref, bias_ref, out_ref, basis, mixed, result, flat_first, turned):
    degrees, bins, channels = first_ref.shape
    width = ext_ref.shape[2]
    shell = lax.axis_index("shell")
    outs, rows, _ = out_ref.shape
    half = rows // 2
    reach = degrees - 1
    need = half + 2 * reach
    lead = EDGE - 2 * reach
    base = EDGE - reach

    flat_first[...] = jnp.zeros_like(flat_first)
    for h in range(2):
        span = slice(h * channels, (h + 1) * channels)
        for k in range(degrees):
            row = (2 * k + h) * bins
            flat_first[row:row + bins, span] = first_ref[k].astype(jnp.float32)
        rest = lift_ref[...]
        for part in range(3):
            row = 2 * bins * degrees + part
            high = rest.astype(jnp.bfloat16).astype(jnp.float32)
            flat_first[row:row + 1, span] = high
            rest = rest - high
    w1 = flat_first[...].T.astype(jnp.bfloat16)
    lanes = lax.broadcasted_iota(jnp.int32, (outs, 2 * channels), 1)
    pieces = []
    for k in range(degrees):
        across = second_ref[k].astype(jnp.float32).T
        turned[k] = jnp.concatenate([across, across], axis=1)
        mine = turned[k, pl.ds(pl.multiple_of(shell * outs, outs), outs), :]
        pieces.append(jnp.where(lanes < channels, mine, 0.0))
        pieces.append(jnp.where(lanes < channels, 0.0, mine))
    w2 = jnp.concatenate(pieces, axis=0).astype(jnp.bfloat16)

    def lateral(field):
        flat = field.reshape(-1, width)
        lane = lax.broadcasted_iota(jnp.int32, flat.shape, 1)
        right = jnp.where(lane == width - 1, 0.0, pltpu.roll(flat, width - 1, 1))
        left = jnp.where(lane == 0, 0.0, pltpu.roll(flat, 1, 1))
        return (right + left).reshape(field.shape)

    for start in range(0, half + 2 * EDGE, 8):
        pieces = []
        for h in range(2):
            for b in range(bins):
                first = h * half + start
                low = first // 16 * 16
                tall = ext_ref[b, low:low + 16, :].astype(jnp.float32)
                pieces.append(tall[first - low:first - low + 8])
        basis[0, start:start + 8] = jnp.swapaxes(jnp.stack(pieces), 0, 1)

    step = 2
    for k in range(1, degrees):
        first = lead + k
        last = first + half + 4 * reach - 2 * k
        for r in range(first, last, step):
            n = min(step, last - r)
            total = basis[k - 1, r - 1:r - 1 + n] + basis[k - 1, r + 1:r + 1 + n] + lateral(basis[k - 1, r:r + n])
            if k == 1:
                basis[k, r:r + n] = -0.25 * total
            else:
                basis[k, r:r + n] = -0.5 * total - basis[k - 2, r:r + n]

    ones = jnp.ones((16, width), jnp.float32)
    deep = w2.shape[0] // degrees

    def mix(pair):
        columns = []
        for q in range(2):
            row = base + 2 * pair + q
            columns.append(jnp.concatenate([basis[k, row] for k in range(degrees)] + [ones], axis=0))
        operand = jnp.concatenate(columns, axis=1).astype(jnp.bfloat16)
        hidden = jnp.dot(w1, operand, preferred_element_type=jnp.float32)
        hidden = jnp.maximum(hidden, 0.0).astype(jnp.bfloat16)
        u = jnp.dot(w2, hidden, preferred_element_type=jnp.float32)
        for q in range(2):
            for k in range(degrees):
                mixed[k, 2 * pair + q] = u[k * deep:(k + 1) * deep, q * width:(q + 1) * width]

    def clenshaw(k, r):
        total = mixed[k + 1, r - 1] + mixed[k + 1, r + 1] + lateral(mixed[k + 1, r])
        value = mixed[k, r] - 0.5 * total
        if k + 2 < degrees:
            value = value - mixed[k + 2, r]
        mixed[k, r] = value

    def finish(block):
        values = []
        for i in range(8):
            r = reach + block * 8 + i
            total = mixed[1, r - 1] + mixed[1, r + 1] + lateral(mixed[1, r])
            values.append(mixed[0, r] - 0.25 * total - mixed[2, r])
        stacked = jnp.stack(values)
        for h in range(2):
            start = h * half + block * 8
            result[:, start:start + 8, :] = jnp.swapaxes(stacked[:, h * outs:(h + 1) * outs], 0, 1)

    ready = {k: reach - k for k in range(degrees)}
    finished = 0
    for pair in range(need // 2):
        mix(pair)
        ready[reach] = 2 * pair + 2
        for k in range(reach - 1, 0, -1):
            while ready[k] + 1 < ready[k + 1]:
                clenshaw(k, ready[k])
                ready[k] += 1
        while finished < half // 8 and reach + finished * 8 + 8 < ready[1]:
            finish(finished)
            finished += 1

    for o in range(outs):
        out_ref[o] = (result[o] + bias_ref[shell * outs + o]).astype(jnp.bfloat16)


def per_device(
    density, kernel_table, shell_row, theta_first, bias_first, theta_second, bias_second
):
    degrees, bins, channels = theta_first.shape
    groups = lax.axis_size("shell")
    rows, width = density.shape[1:]
    outs = theta_second.shape[2] // groups
    ext = exchange(density, kernel_table, shell_row)
    half = rows // 2
    need = half + 2 * (degrees - 1)
    vmem = pl.BlockSpec(memory_space=pltpu.VMEM)
    return pl.pallas_call(
        conv_kernel,
        out_shape=jax.ShapeDtypeStruct((outs, rows, width), jnp.bfloat16),
        in_specs=[vmem, vmem, vmem, vmem, pl.BlockSpec(memory_space=pltpu.SMEM)],
        out_specs=vmem,
        scratch_shapes=[
            pltpu.VMEM((degrees, half + 2 * EDGE, 2 * bins, width), jnp.float32),
            pltpu.VMEM((degrees, need, 2 * outs, width), jnp.float32),
            pltpu.VMEM((outs, rows, width), jnp.float32),
            pltpu.VMEM((2 * bins * degrees + 16, 2 * channels), jnp.float32),
            pltpu.VMEM((degrees, channels, 2 * channels), jnp.float32),
        ],
        compiler_params=pltpu.CompilerParams(vmem_limit_bytes=28 * 2**20),
    )(ext, theta_first, bias_first.reshape(1, channels), theta_second, bias_second)


def solution(mesh):
    return jax.shard_map(
        per_device,
        mesh=mesh,
        in_specs=(P("shell", "sky", None), P(), P("shell"), P(), P(), P(), P()),
        out_specs=P("shell", "sky", None),
        check_vma=False,
    )
```
